256 devices in a mesh: blk: 4 (over y_hi, core), pairs: 64 (over y_lo, x, z).
Axes of the slice: x: 4, y: 4 (y_hi: 2, y_lo: 2; y = y_hi * 2 + y_lo), z: 8, core: 2. Of those that a mesh axis runs over, the one named last changes fastest.
Arguments:
- amplitudes: float32 [256, 1024, 1024], P(('blk', 'pairs')), may hold values from -6 to 6
- domain: int32 [256, 16], P(('blk', 'pairs')), may hold values from 0 to 31, as said below
- counts: int32 [256], P(('blk', 'pairs')), may hold values from 1 to 16, as said below
- integrals: float32 [2048, 2048], P('pairs', 'blk'), may hold values from -0.1875 to 0.1875
Outputs:
- cycle_term: float32 [256, 1024, 1024], P(('blk', 'pairs'))
The draws below stay inside these ranges and needn't reach their ends.
Inputs may be any that keep to these rules, and one draw needn't show every extreme that they name: `domain`: each row holds 16 different tile numbers. The live tiles of pair p are the first counts[p] of its domain; some pair has all 16 live.
All inputs are finite; a program needn't handle non-finite values.
Results may differ from the reference program's by a relative error of at most 0.0003.
Values sent between devices are 32-bit elements; how exact they have to be, the bound alone decides.
No kernel may reach another device: no remote copies, remote signals or barrier semaphores. Data moves between devices by JAX's collectives and lax.ppermute only.
A program may use at most 128 MiB of HBM per device.

```python
import jax
import jax.numpy as jnp
from jax import lax

V = 2048
TILE = 64
DOM = 16
NT = 32
DV = 1024
PAIRS = 256


def draw_domain(key, part):
    key = jax.random.fold_in(key, 11)
    row_keys = jax.random.split(key, PAIRS)

    def single_row(row_key):
        return jax.random.permutation(row_key, NT)[:DOM].astype(jnp.int32)
    return jax.vmap(single_row)(row_keys)


def draw_counts(key, part):
    key = jax.random.fold_in(key, 23)
    values = jax.random.randint(key, (PAIRS,), 1, DOM + 1).astype(jnp.int32)
    return values.at[0].set(DOM)


def block_levels(own_key, shape, cuts, low, top_value):
    def one(dim, parts):
        draws = jax.random.uniform(jax.random.fold_in(jax.random.fold_in(own_key, 6), dim), (parts,), jnp.float32, low / len(cuts), top_value / len(cuts))
        return jnp.repeat(jnp.exp(draws), shape[dim] // parts).reshape((-1,) + (1,) * (len(shape) - dim - 1))

    factor_of = one(*cuts[0])
    for cut in cuts[1:]:
        factor_of = factor_of * one(*cut)
    return factor_of


def bell_draw(stream_key, extent, width, limit, pieces=(), held_as=jnp.bfloat16):
    array = jax.random.normal(stream_key, extent, jnp.float32) * width
    if len(pieces) > 0:
        array = block_levels(stream_key, extent, pieces, -0.22, 0.18) * array
    return jnp.clip(array, min=-limit, max=limit).astype(held_as)


def setup_inputs(seed: int = 0) -> dict:
    streams_of = jax.random.split(jax.random.key(seed), 5)
    amplitudes = bell_draw(streams_of[0], (PAIRS, DV, DV), 1.0, 6.0, ((0, 256),), jnp.float32)
    domain = draw_domain(jax.random.fold_in(streams_of[4], 71), 0)
    counts = draw_counts(jax.random.fold_in(streams_of[4], 71), 0)
    integrals = bell_draw(streams_of[3], (V, V), DV ** -0.5, 0.1875, ((0, 64), (1, 4)), jnp.float32)
    return {"amplitudes": amplitudes, "domain": domain, "counts": counts, "integrals": integrals}


def reference(amplitudes, domain, counts, integrals):
    def single_pair(operands):
        amplitude_block, tiles_of, tile_count = operands
        orbitals = (tiles_of[:, None] * TILE + jnp.arange(TILE, dtype=jnp.int32)[None, :]).reshape(-1).astype(jnp.int32)
        live_mask = jnp.repeat(jnp.arange(DOM, dtype=jnp.int32) < tile_count, TILE).astype(jnp.float32)
        block_rows = jnp.take(integrals, orbitals, axis=0)
        block_part = jnp.take(block_rows, orbitals, axis=1)
        product = jnp.dot(amplitude_block * live_mask[None, :], block_part, precision=lax.Precision.HIGHEST, preferred_element_type=jnp.float32)
        return product * live_mask[:, None] * live_mask[None, :]

    return lax.map(single_pair, (amplitudes, domain, counts))
```

```python
import functools
import itertools

import jax
import jax.numpy as jnp
import numpy as np
from jax import lax
from jax.experimental import pallas as pl
from jax.experimental.pallas import tpu as pltpu
from jax.sharding import Mesh, PartitionSpec as P

AXES = ("yh", "core", "yl", "x", "z")
SIZES = (2, 2, 2, 4, 8)
ANY = pl.BlockSpec(memory_space=pl.ANY)
SMEM = pl.BlockSpec(memory_space=pltpu.SMEM)


def moved(**shift):
    pairs = []
    for at in itertools.product(*(range(n) for n in SIZES)):
        yh, core, yl, x, z = at
        y = (yh * 2 + yl + shift.get("y", 0)) % 4
        to = (
            y // 2,
            (core + shift.get("core", 0)) % 2,
            y % 2,
            (x + shift.get("x", 0)) % 4,
            (z + shift.get("z", 0)) % 8,
        )
        pairs.append((int(np.ravel_multi_index(at, SIZES)), int(np.ravel_multi_index(to, SIZES))))
    return pairs


def fetch(array, **offset):
    return lax.ppermute(array, AXES, moved(**{k: -v for k, v in offset.items()}))


def place(pieces, slots, shape, cost):
    count = len(pieces)
    width = slots.shape[1]

    def kernel(slots_ref, *refs):
        ins, out, sem = refs[:count], refs[count], refs[count + 1]
        copies = []
        for i in range(count):
            at = tuple(slots_ref[i, j] for j in range(width))
            copies.append(pltpu.make_async_copy(ins[i], out.at[at], sem.at[i]))
        for copy in copies:
            copy.start()
        for copy in copies:
            copy.wait()

    return pl.pallas_call(
        kernel,
        out_shape=jax.ShapeDtypeStruct(shape, jnp.float32),
        in_specs=[SMEM] + [ANY] * count,
        out_specs=ANY,
        scratch_shapes=[pltpu.SemaphoreType.DMA((count,))],
        cost_estimate=pl.CostEstimate(flops=0, bytes_accessed=cost, transcendentals=0),
    )(slots, *pieces)


def split_kernel(count_ref, a_ref, hi_ref, lo_ref):
    rows, columns = a_ref.shape
    live = count_ref[0] * 64
    row = lax.broadcasted_iota(jnp.int32, (rows, columns), 0) + pl.program_id(0) * rows
    column = lax.broadcasted_iota(jnp.int32, (rows, columns), 1)
    a = jnp.where((row < live) & (column < live), a_ref[...], 0.0)
    hi = a.astype(jnp.bfloat16)
    hi_ref[...] = hi
    lo_ref[...] = (a - hi.astype(jnp.float32)).astype(jnp.bfloat16)


def split(counts, a):
    return pl.pallas_call(
        split_kernel,
        grid=(8,),
        in_specs=[SMEM, pl.BlockSpec((128, 1024), lambda i: (i, 0))],
        out_specs=[pl.BlockSpec((128, 1024), lambda i: (i, 0))] * 2,
        out_shape=[jax.ShapeDtypeStruct((1024, 1024), jnp.bfloat16)] * 2,
        cost_estimate=pl.CostEstimate(flops=4 << 20, bytes_accessed=8 << 20, transcendentals=0),
    )(counts, a)


def product_kernel(dom, cnt, here, ahi_hbm, alo_hbm, *refs):
    pieces, out_ref, (ahi, alo, raw, b, sem) = refs[:20], refs[20], refs[21:]
    step = pl.program_id(0)
    core, y_me, x_me = here[0], here[1], here[2]

    def build(n, slot):
        lane = lax.broadcasted_iota(jnp.int32, (256, 128), 1)
        for m in range(2):
            first, second = n * 4 + m * 2, n * 4 + m * 2 + 1
            c0, c1 = dom[first], dom[second]
            l0, l1 = lax.div(c0, 2), lax.div(c1, 2)

            def read(l, rows):
                group = lax.div(l, 4)
                at = pl.multiple_of(lax.rem(l, 2) * 128, 128)
                return raw[lax.rem(group, 2), lax.rem(lax.div(l, 2), 2), lax.div(group, 2), rows, pl.ds(at, 128)]

            turn0 = lax.rem(c0, 2) * 64
            turn1 = 64 - lax.rem(c1, 2) * 64
            live0 = (first < cnt[0]).astype(jnp.int32) * 64
            live1 = 64 + (second < cnt[0]).astype(jnp.int32) * 64
            keep = (lane < live0) | ((lane >= 64) & (lane < live1))
            for r in range(0, 1024, 256):
                rows = pl.ds(r, 256)
                left = pltpu.roll(read(l0, rows), turn0, 1)
                right = pltpu.roll(read(l1, rows), turn1, 1)
                value = jnp.where(keep, jnp.where(lane < 64, left, right), 0.0)
                hi = value.astype(jnp.bfloat16)
                b[slot, 0, rows, pl.ds(m * 128, 128)] = hi
                b[slot, 1, rows, pl.ds(m * 128, 128)] = (value - hi.astype(jnp.float32)).astype(jnp.bfloat16)

    @pl.when(step == 0)
    def _():
        pltpu.make_async_copy(ahi_hbm, ahi, sem.at[1]).start()
        pltpu.make_async_copy(alo_hbm, alo, sem.at[2]).start()

        def tile(k, _):
            t = dom[k]
            yl, x, q = lax.div(t, 16), lax.rem(lax.div(t, 4), 4), lax.rem(t, 4)
            to = pl.ds(pl.multiple_of(k * 64, 64), 64)
            dx = lax.rem(x - x_me + 4, 4)
            from_x = pl.ds(pl.multiple_of((yl * 8 + q * 2) * 32, 64), 64)
            from_y = pl.ds(pl.multiple_of((x * 8 + q * 2) * 32, 64), 64)
            for c in range(2):
                at = core if c == 0 else 1 - core
                X, Y = pieces[c * 10 : c * 10 + 5], pieces[c * 10 + 5 : c * 10 + 10]
                for i, d in enumerate((0, 1, 3)):

                    @pl.when(dx == d)
                    def _():
                        pltpu.make_async_copy(X[i].at[:, from_x, :], raw.at[at, 0, :, to, :], sem.at[0]).start()

                @pl.when(dx == 2)
                def _():
                    for h in range(2):
                        pltpu.make_async_copy(X[3 + h].at[from_x, :], raw.at[at, 0, h, to, :], sem.at[0]).start()

                for yh in range(2):
                    dy = lax.rem(yh * 2 + yl - y_me + 4, 4)
                    for i, d in enumerate((0, 1, 3)):

                        @pl.when(dy == d)
                        def _():
                            pltpu.make_async_copy(Y[i].at[from_y, :], raw.at[at, 1, yh, to, :], sem.at[0]).start()

                    for h in range(2):

                        @pl.when((dy == 2) & (lax.div(x, 2) == h))
                        def _():
                            rows = pl.ds(pl.multiple_of(((x - 2 * h) * 8 + q * 2) * 32, 64), 64)
                            pltpu.make_async_copy(Y[3 + h].at[rows, :], raw.at[at, 1, yh, to, :], sem.at[0]).start()

            return 0

        lax.fori_loop(0, 16, tile, 0)
        pltpu.make_async_copy(raw, raw, sem.at[0]).wait()
        build(0, 0)
        pltpu.make_async_copy(ahi_hbm, ahi, sem.at[1]).wait()
        pltpu.make_async_copy(alo_hbm, alo, sem.at[2]).wait()

    slot = lax.rem(step, 2)
    for r in range(0, 1024, 256):
        rows = pl.ds(r, 256)
        total = jnp.dot(ahi[rows, :], b[slot, 0], preferred_element_type=jnp.float32)
        total += jnp.dot(ahi[rows, :], b[slot, 1], preferred_element_type=jnp.float32)
        total += jnp.dot(alo[rows, :], b[slot, 0], preferred_element_type=jnp.float32)
        out_ref[rows, :] = total
    build(lax.rem(step + 1, 4), 1 - slot)


def product(dom, cnt, here, ahi, alo, pieces):
    return pl.pallas_call(
        product_kernel,
        grid=(4,),
        in_specs=[SMEM] * 3 + [ANY] * 22,
        out_specs=pl.BlockSpec((1024, 256), lambda n: (0, n)),
        out_shape=jax.ShapeDtypeStruct((1024, 1024), jnp.float32),
        scratch_shapes=[
            pltpu.VMEM((1024, 1024), jnp.bfloat16),
            pltpu.VMEM((1024, 1024), jnp.bfloat16),
            pltpu.VMEM((2, 2, 2, 1024, 256), jnp.float32),
            pltpu.VMEM((2, 2, 1024, 256), jnp.bfloat16),
            pltpu.SemaphoreType.DMA((3,)),
        ],
        compiler_params=pltpu.CompilerParams(vmem_limit_bytes=40 << 20),
        cost_estimate=pl.CostEstimate(flops=6 << 30, bytes_accessed=20 << 20, transcendentals=0),
    )(dom, cnt, here, ahi, alo, *pieces)


def shards(amplitudes, domain, counts, integrals):
    yh, core, yl, x, z = (lax.axis_index(a).astype(jnp.int32) for a in AXES)
    y = yh * 2 + yl
    i32 = functools.partial(jnp.asarray, dtype=jnp.int32)

    ahi, alo = split(counts, amplitudes[0])

    got = {0: integrals}
    for d in (1, -1, 2, -2):
        got[d] = fetch(integrals, z=d)
    got[3] = fetch(got[2], z=1)
    got[-3] = fetch(got[-2], z=-1)
    top, low = fetch(got[2][:16], z=2), fetch(got[-2][16:], z=-2)
    got[4] = jnp.concatenate([top, low], axis=0)
    order = (0, 1, -1, 2, -2, 3, -3, 4)
    slots = jnp.stack([lax.rem(z + d + 8, 8) for d in order]).reshape(8, 1)
    X = place([got[d][:, :256] for d in order], slots, (8, 32, 256), 1 << 20)
    Y = place([got[d][:, 256:] for d in order], slots, (8, 32, 256), 1 << 20)

    near = (0, 1, 2, 3)
    Xs = [X] + [fetch(X, y=d) for d in (1, 2, 3)]
    Ys = [Y] + [fetch(Y, x=d) for d in (1, 2, 3)]
    slots = jnp.stack([jnp.stack([lax.div(lax.rem(y + d, 4), 2), lax.rem(y + d, 2)]) for d in near])
    X = place(Xs, slots, (2, 2, 8, 32, 256), 4 << 20)
    slots = jnp.stack([lax.rem(x + d, 4) for d in near]).reshape(4, 1)
    Y = place(Ys, slots, (4, 8, 32, 256), 4 << 20)

    X = X.reshape(2, 512, 256)
    Y = Y.reshape(1024, 256)
    Xr, Xl = fetch(X, x=1), fetch(X, x=-1)
    Yr, Yl = fetch(Y, y=1), fetch(Y, y=-1)
    X0, X1 = fetch(Xl[0], x=-1), fetch(Xr[1], x=1)
    Y0, Y1 = fetch(Yl[:512], y=-1), fetch(Yr[512:], y=1)
    own = [X, Xr, Xl, X0, X1, Y, Yr, Yl, Y0, Y1]
    other = [fetch(piece, core=1) for piece in own]

    here = jnp.stack([core, y, x])
    return product(domain[0], counts, here, ahi, alo, own + other)[None]


def solution(mesh):
    fine = Mesh(mesh.devices.reshape(SIZES), AXES)
    whole = P(AXES, None, None)
    return jax.shard_map(
        shards,
        mesh=fine,
        in_specs=(whole, P(AXES, None), P(AXES), P(("yl", "x", "z"), ("yh", "core"))),
        out_specs=whole,
        check_vma=False,
    )
```

```python
import functools
import itertools

import jax
import jax.numpy as jnp
import numpy as np
from jax import lax
from jax.experimental import pallas as pl
from jax.experimental.pallas import tpu as pltpu
from jax.sharding import Mesh, PartitionSpec as P

AXES = ("yh", "core", "yl", "x", "z")
SIZES = (2, 2, 2, 4, 8)
ANY = pl.BlockSpec(memory_space=pl.ANY)
VMEM = pl.BlockSpec(memory_space=pltpu.VMEM)
SMEM = pl.BlockSpec(memory_space=pltpu.SMEM)


def moved(shifts):
    pairs = []
    for at in itertools.product(*(range(n) for n in SIZES)):
        yh, core, yl, x, z = at
        shift = shifts[core]
        y = (yh * 2 + yl + shift.get("y", 0)) % 4
        to = (
            y // 2,
            (core + shift.get("core", 0)) % 2,
            y % 2,
            (x + shift.get("x", 0)) % 4,
            (z + shift.get("z", 0)) % 8,
        )
        pairs.append((int(np.ravel_multi_index(at, SIZES)), int(np.ravel_multi_index(to, SIZES))))
    return pairs


def coordinates():
    yh, core, yl, x, z = (lax.axis_index(a) for a in AXES)
    return core, yh * 2 + yl, x, z


def fetch(array, axes, d):
    return lax.ppermute(array, AXES, moved([{axis: -d} for axis in axes]))


def params(mib):
    return pltpu.CompilerParams(vmem_limit_bytes=mib << 20)


def by_z(got):
    def kernel(*refs):
        ins, upper, lower = refs[:9], refs[9], refs[10]
        z = coordinates()[3]
        for i, d in enumerate((0, 1, -1, 2, -2, 3, -3)):
            at = (z + d) & 7
            upper[at] = ins[i][:16]
            lower[at] = ins[i][16:]
        at = (z + 4) & 7
        upper[at] = ins[7][...]
        lower[at] = ins[8][...]

    return pl.pallas_call(
        kernel,
        out_shape=[jax.ShapeDtypeStruct((8, 16, 512), jnp.float32)] * 2,
        in_specs=[VMEM] * 9,
        out_specs=[VMEM] * 2,
        compiler_params=params(2),
        cost_estimate=pl.CostEstimate(flops=0, bytes_accessed=1 << 20, transcendentals=0),
    )(*got)


def by_yx(pieces):
    def kernel(*refs):
        ins, outs = refs[:8], refs[8:]
        mine = (coordinates()[3] & 1) * 4

        def every(n, _):
            for i in range(8):
                outs[i // 4][i // 2 % 2, i % 2, n] = ins[i][n]
            return 0

        def half(n, _):
            for i in range(8):
                outs[2 + i // 4][i // 2 % 2, i % 2, n] = ins[i][mine + n]
            return 0

        lax.fori_loop(0, 8, every, 0)
        lax.fori_loop(0, 4, half, 0)

    return pl.pallas_call(
        kernel,
        out_shape=[jax.ShapeDtypeStruct((2, 2, n, 16, 512), jnp.float32) for n in (8, 8, 4, 4)],
        in_specs=[VMEM] * 8,
        out_specs=[VMEM] * 4,
        compiler_params=params(2),
        cost_estimate=pl.CostEstimate(flops=0, bytes_accessed=4 << 20, transcendentals=0),
    )(*pieces)


def split_kernel(count_ref, a_ref, hi_ref, lo_ref):
    live = count_ref[0] * 64
    column = lax.broadcasted_iota(jnp.int32, (64, 1024), 1)

    def step(i, _):
        rows = pl.ds(pl.multiple_of(i * 64, 64), 64)
        keep = column < jnp.where(i * 64 < live, live, 0)
        a = jnp.where(keep, a_ref[rows, :], 0.0)
        hi = a.astype(jnp.bfloat16)
        hi_ref[rows, :] = hi
        lo_ref[rows, :] = (a - hi.astype(jnp.float32)).astype(jnp.bfloat16)
        return 0

    lax.fori_loop(0, 16, step, 0)


def split(counts, a):
    return pl.pallas_call(
        split_kernel,
        in_specs=[SMEM, VMEM],
        out_specs=[VMEM] * 2,
        out_shape=[jax.ShapeDtypeStruct((1024, 1024), jnp.bfloat16)] * 2,
        compiler_params=params(2),
        cost_estimate=pl.CostEstimate(flops=4 << 20, bytes_accessed=8 << 20, transcendentals=0),
    )(counts, a)


PIECES = (
    (0, 0, None),
    (0, 1, None),
    (3, 0, None),
    (1, 1, None),
    (1, 0, True),
    (3, 1, True),
    (1, 0, False),
    (3, 1, False),
    (2, 0, None),
    (2, 1, None),
)


def collect(pieces, kinds, dom, slot_of, raw):
    core, y_me, x_me, z_me = coordinates()
    for t in range(32):
        slot_of[t] = 16
    for k in range(16):
        slot_of[dom[k]] = k
    for piece, (other, i) in zip(pieces, kinds):
        away, pair, mine = PIECES[i]
        at = 1 - core if other else core
        far = (jnp.where(at == 0, x_me, y_me) + away) & 3
        first_q = 0 if mine is None else 2 * (z_me & 1 if mine else 1 - (z_me & 1))

        def tiles(n, _):
            for m in range(2):
                major = (jnp.where(at == 0, y_me, x_me) + 2 * pair + m) & 3
                y, x = jnp.where(at == 0, major, far), jnp.where(at == 0, far, major)
                to = slot_of[(y & 1) * 16 + x * 4 + n + first_q] * 64
                for s in range(2):
                    for h in range(2):
                        rows = pl.ds(pl.multiple_of(to + s * 32 + h * 16, 16), 16)
                        raw[at, y >> 1, rows, :] = piece[m, h, n * 2 + s]
            return 0

        lax.fori_loop(0, piece.shape[2] // 2, tiles, 0)


def product_kernel(kinds, dom, cnt, ahi, alo, *refs):
    count = len(kinds)
    pieces, out_hbm, (raw, b, out, slot_of, sem) = refs[:count], refs[count], refs[count + 1 :]

    def build(n, slot, rows):
        for m in range(2):
            first = n * 4 + m * 2
            c0, c1 = dom[first], dom[first + 1]

            def read(c):
                group, at = c >> 3, pl.multiple_of(((c >> 1) & 3) * 128, 128)
                return raw[group & 1, group >> 1, rows, pl.ds(at, 128)]

            left, right = pltpu.roll(read(c0), (c0 & 1) * 64, 1), pltpu.roll(read(c1), 64 - (c1 & 1) * 64, 1)
            live0, live1 = jnp.where(first < cnt[0], 64, 0), jnp.where(first + 1 < cnt[0], 128, 0)
            lane = lax.broadcasted_iota(jnp.int32, left.shape, 1)
            keep = (lane < live0) | ((lane >= 64) & (lane < live1))
            value = jnp.where(keep, jnp.where(lane < 64, left, right), 0.0)
            hi = value.astype(jnp.bfloat16)
            b[slot, 0, rows, m * 128 : m * 128 + 128] = hi
            b[slot, 1, rows, m * 128 : m * 128 + 128] = (value - hi.astype(jnp.float32)).astype(jnp.bfloat16)

    collect(pieces, kinds, dom, slot_of, raw)

    def first_build(i, _):
        build(0, 0, pl.ds(pl.multiple_of(i * 64, 64), 64))
        return 0

    lax.fori_loop(0, 16, first_build, 0)

    def written(n, slot):
        columns = pl.ds(pl.multiple_of(n * 256, 256), 256)
        return pltpu.make_async_copy(out.at[slot], out_hbm.at[:, columns], sem.at[slot])

    def multiply(n, _):
        slot = n & 1

        @pl.when(n >= 2)
        def _():
            written(n - 2, slot).wait()

        total = jnp.dot(ahi[...], b[slot, 0], preferred_element_type=jnp.float32)
        total += jnp.dot(ahi[...], b[slot, 1], preferred_element_type=jnp.float32)
        total += jnp.dot(alo[...], b[slot, 0], preferred_element_type=jnp.float32)
        out[slot] = total
        build((n + 1) & 3, 1 - slot, pl.ds(0, 1024))
        written(n, slot).start()
        return 0

    lax.fori_loop(0, 4, multiply, 0)
    written(2, 0).wait()
    written(3, 1).wait()


def product(dom, cnt, ahi, alo, pieces, kinds):
    return pl.pallas_call(
        functools.partial(product_kernel, kinds),
        in_specs=[SMEM] * 2 + [VMEM] * (2 + len(pieces)),
        out_specs=ANY,
        out_shape=jax.ShapeDtypeStruct((1024, 1024), jnp.float32),
        scratch_shapes=[
            pltpu.VMEM((2, 2, 1088, 512), jnp.float32),
            pltpu.VMEM((2, 2, 1024, 256), jnp.bfloat16),
            pltpu.VMEM((2, 1024, 256), jnp.float32),
            pltpu.SMEM((32,), jnp.int32),
            pltpu.SemaphoreType.DMA((2,)),
        ],
        compiler_params=params(18),
        cost_estimate=pl.CostEstimate(flops=6 << 30, bytes_accessed=20 << 20, transcendentals=0),
    )(dom, cnt, ahi, alo, *pieces)


def shards(amplitudes, domain, counts, integrals):
    Z = ("z", "z")
    got = {0: integrals}
    for d in (1, -1, 2, -2):
        got[d] = fetch(integrals, Z, d)
    got[3], got[-3] = fetch(got[2], Z, 1), fetch(got[-2], Z, -1)
    top, low = fetch(got[2][:16], Z, 2), fetch(got[-2][16:], Z, -2)
    A, B = by_z([got[d] for d in (0, 1, -1, 2, -2, 3, -3)] + [top, low])

    YX = ("y", "x")
    a3, b1 = fetch(A, YX, -1), fetch(B, YX, 1)
    a1, b3 = fetch(A, YX, 1), fetch(B, YX, -1)
    a2, b2 = fetch(a3, YX, -1), fetch(b1, YX, 1)

    first, second, first_mine, second_mine = by_yx([A, B, a1, b1, a2, b2, a3, b3])

    XY = ("x", "y")
    first3, second1 = fetch(first, XY, -1), fetch(second, XY, 1)
    first1, second3 = fetch(first_mine, XY, 1), fetch(second_mine, XY, -1)
    swap = lambda piece: lax.ppermute(piece, AXES, moved([{"core": 1}] * 2))
    other_first = swap(first)
    first3, second1, first1, second3, other_first, amplitudes = lax.optimization_barrier(
        (first3, second1, first1, second3, other_first, amplitudes)
    )
    first2, second2 = fetch(first3, XY, -1), fetch(second1, XY, 1)
    first1_rest, second3_rest = fetch(first1, Z, 1), fetch(second3, Z, -1)
    ahi, alo = split(counts, amplitudes[0])
    first1_rest, second3_rest, ahi, alo = lax.optimization_barrier((first1_rest, second3_rest, ahi, alo))
    own = [first, second, first3, second1, first1, second3, first1_rest, second3_rest, first2, second2]
    other = [other_first] + [swap(piece) for piece in own[1:]]
    kinds = [(c, i) for c in range(2) for i in range(10)]
    return product(domain[0], counts, ahi, alo, own + other, kinds)[None]


def solution(mesh):
    fine = Mesh(mesh.devices.reshape(SIZES), AXES)
    whole = P(AXES, None, None)
    return jax.shard_map(
        shards,
        mesh=fine,
        in_specs=(whole, P(AXES, None), P(AXES), P(("yl", "x", "z"), ("yh", "core"))),
        out_specs=whole,
        check_vma=False,
    )
```

```python
import functools
import itertools

import jax
import jax.numpy as jnp
import numpy as np
from jax import lax
from jax.experimental import pallas as pl
from jax.experimental.pallas import tpu as pltpu
from jax.sharding import Mesh, PartitionSpec as P

AXES = ("yh", "core", "yl", "x", "z")
SIZES = (2, 2, 2, 4, 8)
ANY = pl.BlockSpec(memory_space=pl.ANY)
VMEM = pl.BlockSpec(memory_space=pltpu.VMEM)
SMEM = pl.BlockSpec(memory_space=pltpu.SMEM)


def moved(shifts):
    pairs = []
    for at in itertools.product(*(range(n) for n in SIZES)):
        yh, core, yl, x, z = at
        shift = shifts[core]
        y = (yh * 2 + yl + shift.get("y", 0)) % 4
        to = (
            y // 2,
            (core + shift.get("core", 0)) % 2,
            y % 2,
            (x + shift.get("x", 0)) % 4,
            (z + shift.get("z", 0)) % 8,
        )
        pairs.append((int(np.ravel_multi_index(at, SIZES)), int(np.ravel_multi_index(to, SIZES))))
    return pairs


def coordinates():
    yh, core, yl, x, z = (lax.axis_index(a) for a in AXES)
    return core, yh * 2 + yl, x, z


def fetch(array, axes, d):
    return lax.ppermute(array, AXES, moved([{axis: -d} for axis in axes]))


def params(mib):
    return pltpu.CompilerParams(vmem_limit_bytes=mib << 20)


def by_z(got):
    def kernel(*refs):
        ins, upper, lower = refs[:9], refs[9], refs[10]
        z = coordinates()[3]
        for i, d in enumerate((0, 1, -1, 2, -2, 3, -3)):
            at = (z + d) & 7
            upper[at] = ins[i][:16]
            lower[at] = ins[i][16:]
        at = (z + 4) & 7
        upper[at] = ins[7][...]
        lower[at] = ins[8][...]

    return pl.pallas_call(
        kernel,
        out_shape=[jax.ShapeDtypeStruct((8, 16, 512), jnp.float32)] * 2,
        in_specs=[VMEM] * 9,
        out_specs=[VMEM] * 2,
        compiler_params=params(2),
        cost_estimate=pl.CostEstimate(flops=0, bytes_accessed=1 << 20, transcendentals=0),
    )(*got)


def by_yx(pieces):
    def kernel(*refs):
        ins, outs = refs[:8], refs[8:]
        mine = 4 + (coordinates()[3] & 1) * 2

        def every(n, _):
            for i in range(8):
                outs[i // 4][i // 2 % 2, i % 2, n] = ins[i][n]
            return 0

        def some(n, _):
            z = jnp.where(n < 4, n, mine + n - 4)
            for i in range(8):
                outs[2 + i // 4][i // 2 % 2, i % 2, n] = ins[i][z]
            return 0

        lax.fori_loop(0, 8, every, 0)
        lax.fori_loop(0, 6, some, 0)

    return pl.pallas_call(
        kernel,
        out_shape=[jax.ShapeDtypeStruct((2, 2, n, 16, 512), jnp.float32) for n in (8, 8, 6, 6)],
        in_specs=[VMEM] * 8,
        out_specs=[VMEM] * 4,
        compiler_params=params(2),
        cost_estimate=pl.CostEstimate(flops=0, bytes_accessed=4 << 20, transcendentals=0),
    )(*pieces)


def last_z(pieces):
    def kernel(*refs):
        for piece, part in zip(refs[:2], refs[2:]):
            part[...] = piece[:, :, 4:]

    return pl.pallas_call(
        kernel,
        out_shape=[jax.ShapeDtypeStruct((2, 2, 2, 16, 512), jnp.float32)] * 2,
        in_specs=[VMEM] * 2,
        out_specs=[VMEM] * 2,
        compiler_params=params(2),
        cost_estimate=pl.CostEstimate(flops=0, bytes_accessed=1 << 20, transcendentals=0),
    )(*pieces)


def split_kernel(count_ref, a_ref, hi_ref, lo_ref):
    live = count_ref[0] * 64
    column = lax.broadcasted_iota(jnp.int32, (64, 1024), 1)

    def step(i, _):
        rows = pl.ds(pl.multiple_of(i * 64, 64), 64)
        keep = column < jnp.where(i * 64 < live, live, 0)
        a = jnp.where(keep, a_ref[rows, :], 0.0)
        hi = a.astype(jnp.bfloat16)
        hi_ref[rows, :] = hi
        lo_ref[rows, :] = (a - hi.astype(jnp.float32)).astype(jnp.bfloat16)
        return 0

    lax.fori_loop(0, 16, step, 0)


def split(counts, a):
    return pl.pallas_call(
        split_kernel,
        in_specs=[SMEM, VMEM],
        out_specs=[VMEM] * 2,
        out_shape=[jax.ShapeDtypeStruct((1024, 1024), jnp.bfloat16)] * 2,
        compiler_params=params(2),
        cost_estimate=pl.CostEstimate(flops=4 << 20, bytes_accessed=8 << 20, transcendentals=0),
    )(counts, a)


PIECES = (
    (0, 0, None),
    (0, 1, None),
    (3, 0, None),
    (1, 1, None),
    (1, 0, True),
    (3, 1, True),
    (1, 0, False),
    (3, 1, False),
    (2, 0, None),
    (2, 1, None),
)


def collect(pieces, kinds, dom, slot_of, raw):
    core, y_me, x_me, z_me = coordinates()
    for t in range(32):
        slot_of[t] = 16
    for k in range(16):
        slot_of[dom[k]] = k
    for piece, (other, i) in zip(pieces, kinds):
        away, pair, mine = PIECES[i]
        at = 1 - core if other else core
        far = (jnp.where(at == 0, x_me, y_me) + away) & 3
        parity = z_me & 1

        def tiles(n, _):
            q = n if mine is None else jnp.where(n < 2, n, 2 + parity) if mine else 3 - parity
            for m in range(2):
                major = (jnp.where(at == 0, y_me, x_me) + 2 * pair + m) & 3
                y, x = jnp.where(at == 0, major, far), jnp.where(at == 0, far, major)
                to = slot_of[(y & 1) * 16 + x * 4 + q] * 64
                for s in range(2):
                    for h in range(2):
                        rows = pl.ds(pl.multiple_of(to + s * 32 + h * 16, 16), 16)
                        raw[at, y >> 1, rows, :] = piece[m, h, n * 2 + s]
            return 0

        lax.fori_loop(0, piece.shape[2] // 2, tiles, 0)


def product_kernel(kinds, dom, cnt, ahi, alo, *refs):
    count = len(kinds)
    pieces, out_hbm, (raw, b, out, slot_of, sem) = refs[:count], refs[count], refs[count + 1 :]

    def build(n, slot, rows):
        for m in range(2):
            first = n * 4 + m * 2
            c0, c1 = dom[first], dom[first + 1]

            def read(c):
                group, at = c >> 3, pl.multiple_of(((c >> 1) & 3) * 128, 128)
                return raw[group & 1, group >> 1, rows, pl.ds(at, 128)]

            left, right = pltpu.roll(read(c0), (c0 & 1) * 64, 1), pltpu.roll(read(c1), 64 - (c1 & 1) * 64, 1)
            live0, live1 = jnp.where(first < cnt[0], 64, 0), jnp.where(first + 1 < cnt[0], 128, 0)
            lane = lax.broadcasted_iota(jnp.int32, left.shape, 1)
            keep = (lane < live0) | ((lane >= 64) & (lane < live1))
            value = jnp.where(keep, jnp.where(lane < 64, left, right), 0.0)
            hi = value.astype(jnp.bfloat16)
            b[slot, 0, rows, m * 128 : m * 128 + 128] = hi
            b[slot, 1, rows, m * 128 : m * 128 + 128] = (value - hi.astype(jnp.float32)).astype(jnp.bfloat16)

    collect(pieces, kinds, dom, slot_of, raw)

    def first_build(i, _):
        build(0, 0, pl.ds(pl.multiple_of(i * 64, 64), 64))
        return 0

    lax.fori_loop(0, 16, first_build, 0)

    def written(n, slot):
        columns = pl.ds(pl.multiple_of(n * 256, 256), 256)
        return pltpu.make_async_copy(out.at[slot], out_hbm.at[:, columns], sem.at[slot])

    def multiply(n, _):
        slot = n & 1

        @pl.when(n >= 2)
        def _():
            written(n - 2, slot).wait()

        total = jnp.dot(ahi[...], b[slot, 0], preferred_element_type=jnp.float32)
        total += jnp.dot(ahi[...], b[slot, 1], preferred_element_type=jnp.float32)
        total += jnp.dot(alo[...], b[slot, 0], preferred_element_type=jnp.float32)
        out[slot] = total
        build((n + 1) & 3, 1 - slot, pl.ds(0, 1024))
        written(n, slot).start()
        return 0

    lax.fori_loop(0, 4, multiply, 0)
    written(2, 0).wait()
    written(3, 1).wait()


def product(dom, cnt, ahi, alo, pieces, kinds):
    return pl.pallas_call(
        functools.partial(product_kernel, kinds),
        in_specs=[SMEM] * 2 + [VMEM] * (2 + len(pieces)),
        out_specs=ANY,
        out_shape=jax.ShapeDtypeStruct((1024, 1024), jnp.float32),
        scratch_shapes=[
            pltpu.VMEM((2, 2, 1088, 512), jnp.float32),
            pltpu.VMEM((2, 2, 1024, 256), jnp.bfloat16),
            pltpu.VMEM((2, 1024, 256), jnp.float32),
            pltpu.SMEM((32,), jnp.int32),
            pltpu.SemaphoreType.DMA((2,)),
        ],
        compiler_params=params(20),
        cost_estimate=pl.CostEstimate(flops=6 << 30, bytes_accessed=20 << 20, transcendentals=0),
    )(dom, cnt, ahi, alo, *pieces)


def shards(amplitudes, domain, counts, integrals):
    Z = ("z", "z")
    got = {0: integrals}
    for d in (1, -1, 2, -2):
        got[d] = fetch(integrals, Z, d)
    got[3], got[-3] = fetch(got[2], Z, 1), fetch(got[-2], Z, -1)
    top, low = fetch(got[2][:16], Z, 2), fetch(got[-2][16:], Z, -2)
    A, B = by_z([got[d] for d in (0, 1, -1, 2, -2, 3, -3)] + [top, low])

    YX = ("y", "x")
    a3, b1 = fetch(A, YX, -1), fetch(B, YX, 1)
    a1, b3 = fetch(A, YX, 1), fetch(B, YX, -1)
    a2, b2 = fetch(a3, YX, -1), fetch(b1, YX, 1)

    first, second, first_mine, second_mine = by_yx([A, B, a1, b1, a2, b2, a3, b3])

    XY = ("x", "y")
    swap = lambda piece: lax.ppermute(piece, AXES, moved([{"core": 1}] * 2))
    tie = lambda *arrays: lax.optimization_barrier(arrays)
    first3, second1 = fetch(first, XY, -1), fetch(second, XY, 1)
    first1, second3 = fetch(first_mine, XY, 1), fetch(second_mine, XY, -1)
    other_first = swap(first)
    second, other_first = tie(second, other_first)
    other_second = swap(second)
    ahi, alo = split(counts, amplitudes[0])
    first3, second1, other_first, other_second, ahi, alo = tie(first3, second1, other_first, other_second, ahi, alo)
    first2, second2 = fetch(first3, XY, -1), fetch(second1, XY, 1)
    first1, second3, first3, second1 = tie(first1, second3, first3, second1)
    spare1, spare3 = last_z((first1, second3))
    first1_rest, second3_rest = fetch(spare1, Z, 1), fetch(spare3, Z, -1)
    own = [first, second, first3, second1, first1, second3, first1_rest, second3_rest, first2, second2]
    other = [other_first, other_second] + [swap(piece) for piece in own[2:]]
    kinds = [(c, i) for c in range(2) for i in range(10)]
    return product(domain[0], counts, ahi, alo, own + other, kinds)[None]


def solution(mesh):
    fine = Mesh(mesh.devices.reshape(SIZES), AXES)
    whole = P(AXES, None, None)
    return jax.shard_map(
        shards,
        mesh=fine,
        in_specs=(whole, P(AXES, None), P(AXES), P(("yl", "x", "z"), ("yh", "core"))),
        out_specs=whole,
        check_vma=False,
    )
```

```python
import functools
import itertools

import jax
import jax.numpy as jnp
import numpy as np
from jax import lax
from jax.experimental import pallas as pl
from jax.experimental.pallas import tpu as pltpu
from jax.sharding import Mesh, PartitionSpec as P

AXES = ("yh", "core", "yl", "x", "z")
SIZES = (2, 2, 2, 4, 8)
ANY = pl.BlockSpec(memory_space=pl.ANY)
VMEM = pl.BlockSpec(memory_space=pltpu.VMEM)
SMEM = pl.BlockSpec(memory_space=pltpu.SMEM)


def moved(shifts):
    pairs = []
    for at in itertools.product(*(range(n) for n in SIZES)):
        yh, core, yl, x, z = at
        shift = shifts[core]
        y = (yh * 2 + yl + shift.get("y", 0)) % 4
        to = (
            y // 2,
            (core + shift.get("core", 0)) % 2,
            y % 2,
            (x + shift.get("x", 0)) % 4,
            (z + shift.get("z", 0)) % 8,
        )
        pairs.append((int(np.ravel_multi_index(at, SIZES)), int(np.ravel_multi_index(to, SIZES))))
    return pairs


def coordinates():
    yh, core, yl, x, z = (lax.axis_index(a) for a in AXES)
    return core, yh * 2 + yl, x, z


def tie(*arrays):
    return lax.optimization_barrier(arrays)


def fetch(array, axes, d):
    return lax.ppermute(array, AXES, moved([{axis: -d} for axis in axes]))


def params(mib):
    return pltpu.CompilerParams(vmem_limit_bytes=mib << 20)


def by_z(got):
    def kernel(*refs):
        ins, upper, lower = refs[:9], refs[9], refs[10]
        z = coordinates()[3]
        for i, d in enumerate((0, 1, -1, 2, -2, 3, -3)):
            at = (z + d) & 7
            upper[at] = ins[i][:16]
            lower[at] = ins[i][16:]
        at = (z + 4) & 7
        upper[at] = ins[7][...]
        lower[at] = ins[8][...]

    return pl.pallas_call(
        kernel,
        out_shape=[jax.ShapeDtypeStruct((8, 16, 512), jnp.float32)] * 2,
        in_specs=[VMEM] * 9,
        out_specs=[VMEM] * 2,
        compiler_params=params(2),
        cost_estimate=pl.CostEstimate(flops=0, bytes_accessed=1 << 20, transcendentals=0),
    )(*got)


def by_yx(pieces):
    def kernel(*refs):
        ins, outs = refs[:8], refs[8:]
        mine = 4 + (coordinates()[3] & 1) * 2

        def every(n, _):
            for i in range(8):
                outs[i // 4][i // 2 % 2, i % 2, n] = ins[i][n]
            return 0

        def some(n, _):
            z = jnp.where(n < 4, n, mine + n - 4)
            for i in range(8):
                outs[2 + i // 4][i // 2 % 2, i % 2, n] = ins[i][z]
            return 0

        lax.fori_loop(0, 8, every, 0)
        lax.fori_loop(0, 6, some, 0)

    return pl.pallas_call(
        kernel,
        out_shape=[jax.ShapeDtypeStruct((2, 2, n, 16, 512), jnp.float32) for n in (8, 8, 6, 6)],
        in_specs=[VMEM] * 8,
        out_specs=[VMEM] * 4,
        compiler_params=params(2),
        cost_estimate=pl.CostEstimate(flops=0, bytes_accessed=4 << 20, transcendentals=0),
    )(*pieces)


def here(block):
    def kernel(block, out):
        out[...] = block[...]

    return pl.pallas_call(
        kernel,
        out_shape=jax.ShapeDtypeStruct(block.shape, jnp.float32),
        in_specs=[VMEM],
        out_specs=VMEM,
        compiler_params=params(2),
        cost_estimate=pl.CostEstimate(flops=0, bytes_accessed=1 << 17, transcendentals=0),
    )(block)


def last_z(first, second):
    def kernel(first, second, out):
        out[0] = first[:, :, 4:]
        out[1] = second[:, :, 4:]

    return pl.pallas_call(
        kernel,
        out_shape=jax.ShapeDtypeStruct((2, 2, 2, 2, 16, 512), jnp.float32),
        in_specs=[VMEM] * 2,
        out_specs=VMEM,
        compiler_params=params(2),
        cost_estimate=pl.CostEstimate(flops=0, bytes_accessed=1 << 20, transcendentals=0),
    )(first, second)


def split_kernel(count_ref, a_ref, hi_ref, lo_ref):
    live = count_ref[0] * 64
    column = lax.broadcasted_iota(jnp.int32, (64, 1024), 1)

    def step(i, _):
        rows = pl.ds(pl.multiple_of(i * 64, 64), 64)
        keep = column < jnp.where(i * 64 < live, live, 0)
        a = jnp.where(keep, a_ref[rows, :], 0.0)
        hi = a.astype(jnp.bfloat16)
        hi_ref[rows, :] = hi
        lo_ref[rows, :] = (a - hi.astype(jnp.float32)).astype(jnp.bfloat16)
        return 0

    lax.fori_loop(0, 16, step, 0)


def split(counts, a):
    return pl.pallas_call(
        split_kernel,
        in_specs=[SMEM, VMEM],
        out_specs=[VMEM] * 2,
        out_shape=[jax.ShapeDtypeStruct((1024, 1024), jnp.bfloat16)] * 2,
        compiler_params=params(2),
        cost_estimate=pl.CostEstimate(flops=4 << 20, bytes_accessed=8 << 20, transcendentals=0),
    )(counts, a)


PIECES = (
    (0, 0, None),
    (0, 1, None),
    (3, 0, None),
    (1, 1, None),
    (1, 0, True),
    (3, 1, True),
    (1, 0, False),
    (3, 1, False),
    (2, 0, None),
    (2, 1, None),
)


def collect(pieces, kinds, dom, slot_of, raw):
    core, y_me, x_me, z_me = coordinates()
    for t in range(32):
        slot_of[t] = 16
    for k in range(16):
        slot_of[dom[k]] = k
    parts = []
    for piece, (other, *which) in zip(pieces, kinds):
        parts += [(piece.at[n] if len(which) > 1 else piece, other, i) for n, i in enumerate(which)]
    for piece, other, i in parts:
        away, pair, mine = PIECES[i]
        at = 1 - core if other else core
        far = (jnp.where(at == 0, x_me, y_me) + away) & 3
        parity = z_me & 1

        def tiles(n, _):
            q = n if mine is None else jnp.where(n < 2, n, 2 + parity) if mine else 3 - parity
            for m in range(2):
                major = (jnp.where(at == 0, y_me, x_me) + 2 * pair + m) & 3
                y, x = jnp.where(at == 0, major, far), jnp.where(at == 0, far, major)
                to = slot_of[(y & 1) * 16 + x * 4 + q] * 64
                for s in range(2):
                    for h in range(2):
                        rows = pl.ds(pl.multiple_of(to + s * 32 + h * 16, 16), 16)
                        raw[at, y >> 1, rows, :] = piece[m, h, n * 2 + s]
            return 0

        lax.fori_loop(0, piece.shape[2] // 2, tiles, 0)


def collect_early(dom, pieces, kinds):
    def kernel(dom, *refs):
        collect(refs[:-2], kinds, dom, refs[-1], refs[-2])

    return pl.pallas_call(
        kernel,
        in_specs=[SMEM] + [VMEM] * len(pieces),
        out_specs=VMEM,
        out_shape=jax.ShapeDtypeStruct((2, 2, 1088, 512), jnp.float32),
        scratch_shapes=[pltpu.SMEM((32,), jnp.int32)],
        compiler_params=params(2),
        cost_estimate=pl.CostEstimate(flops=0, bytes_accessed=8 << 20, transcendentals=0),
    )(dom, *pieces)


def product_kernel(kinds, dom, cnt, ahi, alo, _, *refs):
    count = len(kinds)
    pieces, out_hbm, raw, (b, out, slot_of, sem) = refs[:count], refs[count], refs[count + 1], refs[count + 2 :]

    def build(n, slot, rows):
        for m in range(2):
            first = n * 4 + m * 2
            c0, c1 = dom[first], dom[first + 1]

            def read(c):
                group, at = c >> 3, pl.multiple_of(((c >> 1) & 3) * 128, 128)
                return raw[group & 1, group >> 1, rows, pl.ds(at, 128)]

            left, right = pltpu.roll(read(c0), (c0 & 1) * 64, 1), pltpu.roll(read(c1), 64 - (c1 & 1) * 64, 1)
            live0, live1 = jnp.where(first < cnt[0], 64, 0), jnp.where(first + 1 < cnt[0], 128, 0)
            lane = lax.broadcasted_iota(jnp.int32, left.shape, 1)
            keep = (lane < live0) | ((lane >= 64) & (lane < live1))
            value = jnp.where(keep, jnp.where(lane < 64, left, right), 0.0)
            hi = value.astype(jnp.bfloat16)
            b[slot, 0, rows, m * 128 : m * 128 + 128] = hi
            b[slot, 1, rows, m * 128 : m * 128 + 128] = (value - hi.astype(jnp.float32)).astype(jnp.bfloat16)

    collect(pieces, kinds, dom, slot_of, raw)

    def first_build(i, _):
        build(0, 0, pl.ds(pl.multiple_of(i * 64, 64), 64))
        return 0

    lax.fori_loop(0, 16, first_build, 0)

    def written(n, slot):
        columns = pl.ds(pl.multiple_of(n * 256, 256), 256)
        return pltpu.make_async_copy(out.at[slot], out_hbm.at[:, columns], sem.at[slot])

    def multiply(n, _):
        slot = n & 1

        @pl.when(n >= 2)
        def _():
            written(n - 2, slot).wait()

        total = jnp.dot(ahi[...], b[slot, 0], preferred_element_type=jnp.float32)
        total += jnp.dot(ahi[...], b[slot, 1], preferred_element_type=jnp.float32)
        total += jnp.dot(alo[...], b[slot, 0], preferred_element_type=jnp.float32)
        out[slot] = total
        build((n + 1) & 3, 1 - slot, pl.ds(0, 1024))
        written(n, slot).start()
        return 0

    lax.fori_loop(0, 4, multiply, 0)
    written(2, 0).wait()
    written(3, 1).wait()


def product(dom, cnt, ahi, alo, raw, pieces, kinds):
    return pl.pallas_call(
        functools.partial(product_kernel, kinds),
        in_specs=[SMEM] * 2 + [VMEM] * (3 + len(pieces)),
        out_specs=[ANY, VMEM],
        out_shape=[jax.ShapeDtypeStruct((1024, 1024), jnp.float32), jax.ShapeDtypeStruct(raw.shape, raw.dtype)],
        scratch_shapes=[
            pltpu.VMEM((2, 2, 1024, 256), jnp.bfloat16),
            pltpu.VMEM((2, 1024, 256), jnp.float32),
            pltpu.SMEM((32,), jnp.int32),
            pltpu.SemaphoreType.DMA((2,)),
        ],
        input_output_aliases={4: 1},
        compiler_params=params(11),
        cost_estimate=pl.CostEstimate(flops=6 << 30, bytes_accessed=20 << 20, transcendentals=0),
    )(dom, cnt, ahi, alo, raw, *pieces)[0]


def shards(amplitudes, domain, counts, integrals):
    Z = ("z", "z")
    got = {0: integrals}
    for d in (1, -1, 2, -2):
        got[d] = fetch(integrals, Z, d)
    got[2], got[-2], got[0] = tie(got[2], got[-2], here(integrals))
    got[3], got[-3] = fetch(got[2], Z, 1), fetch(got[-2], Z, -1)
    top, low = fetch(got[2][:16], Z, 2), fetch(got[-2][16:], Z, -2)
    A, B = by_z([got[d] for d in (0, 1, -1, 2, -2, 3, -3)] + [top, low])

    YX = ("y", "x")
    a3, b1 = fetch(A, YX, -1), fetch(B, YX, 1)
    a1, b3 = fetch(A, YX, 1), fetch(B, YX, -1)
    a2, b2 = fetch(a3, YX, -1), fetch(b1, YX, 1)

    first, second, first_mine, second_mine = by_yx([A, B, a1, b1, a2, b2, a3, b3])

    XY = ("x", "y")
    swap = lambda piece: lax.ppermute(piece, AXES, moved([{"core": 1}] * 2))
    first3, second1 = fetch(first, XY, -1), fetch(second, XY, 1)
    first1, second3 = fetch(first_mine, XY, 1), fetch(second_mine, XY, -1)
    other_first = swap(first)
    second, other_first = tie(second, other_first)
    other_second = swap(second)
    ahi, alo = split(counts, amplitudes[0])
    first3, second1, other_first, other_second, ahi, alo = tie(first3, second1, other_first, other_second, ahi, alo)
    first2, second2 = fetch(first3, XY, -1), fetch(second1, XY, 1)
    first1, second3, first3, second1 = tie(first1, second3, first3, second1)
    rest = lax.ppermute(last_z(first1, second3), AXES, moved([{"z": -1}, {"z": 1}]))

    own = [first, second, first3, second1, first1, second3]
    other = [other_first, other_second] + [swap(piece) for piece in own[2:]]
    early = [(0, i) for i in range(6)] + [(1, i) for i in range(4)]
    raw = collect_early(domain[0], own + other[:4], early)
    last = [rest, first2, second2]
    late = [(1, 4), (1, 5)] + [(c, *which) for c in range(2) for which in ((6, 7), (8,), (9,))]
    return product(domain[0], counts, ahi, alo, raw, other[4:] + last + [swap(piece) for piece in last], late)[None]


def solution(mesh):
    fine = Mesh(mesh.devices.reshape(SIZES), AXES)
    whole = P(AXES, None, None)
    return jax.shard_map(
        shards,
        mesh=fine,
        in_specs=(whole, P(AXES, None), P(AXES), P(("yl", "x", "z"), ("yh", "core"))),
        out_specs=whole,
        check_vma=False,
    )
```

```python
import functools
import itertools

import jax
import jax.numpy as jnp
import numpy as np
from jax import lax
from jax.experimental import pallas as pl
from jax.experimental.pallas import tpu as pltpu
from jax.sharding import Mesh, PartitionSpec as P

AXES = ("yh", "core", "yl", "x", "z")
SIZES = (2, 2, 2, 4, 8)
ANY = pl.BlockSpec(memory_space=pl.ANY)
VMEM = pl.BlockSpec(memory_space=pltpu.VMEM)
SMEM = pl.BlockSpec(memory_space=pltpu.SMEM)


def moved(shifts):
    pairs = []
    for at in itertools.product(*(range(n) for n in SIZES)):
        yh, core, yl, x, z = at
        shift = shifts[core]
        y = (yh * 2 + yl + shift.get("y", 0)) % 4
        to = (
            y // 2,
            (core + shift.get("core", 0)) % 2,
            y % 2,
            (x + shift.get("x", 0)) % 4,
            (z + shift.get("z", 0)) % 8,
        )
        pairs.append((int(np.ravel_multi_index(at, SIZES)), int(np.ravel_multi_index(to, SIZES))))
    return pairs


def coordinates():
    yh, core, yl, x, z = (lax.axis_index(a) for a in AXES)
    return core, yh * 2 + yl, x, z


def tie(*arrays):
    return lax.optimization_barrier(arrays)


def fetch(array, axes, d):
    return lax.ppermute(array, AXES, moved([{axis: -d} for axis in axes]))


def params(mib):
    return pltpu.CompilerParams(vmem_limit_bytes=mib << 20)


def by_z(got):
    def kernel(*refs):
        ins, upper, lower = refs[:9], refs[9], refs[10]
        z = coordinates()[3]
        for i, d in enumerate((0, 1, -1, 2, -2, 3, -3)):
            at = (z + d) & 7
            upper[at] = ins[i][:16]
            lower[at] = ins[i][16:]
        at = (z + 4) & 7
        upper[at] = ins[7][...]
        lower[at] = ins[8][...]

    return pl.pallas_call(
        kernel,
        out_shape=[jax.ShapeDtypeStruct((8, 16, 512), jnp.float32)] * 2,
        in_specs=[VMEM] * 9,
        out_specs=[VMEM] * 2,
        compiler_params=params(2),
        cost_estimate=pl.CostEstimate(flops=0, bytes_accessed=1 << 20, transcendentals=0),
    )(*got)


def by_yx(pieces):
    def kernel(*refs):
        ins, outs = refs[:8], refs[8:]
        mine = 4 + (coordinates()[3] & 1) * 2

        def every(n, _):
            for i in range(8):
                outs[i // 4][i // 2 % 2, i % 2, n] = ins[i][n]
            return 0

        def some(n, _):
            z = jnp.where(n < 4, n, mine + n - 4)
            for i in range(8):
                outs[2 + i // 4][i // 2 % 2, i % 2, n] = ins[i][z]
            return 0

        lax.fori_loop(0, 8, every, 0)
        lax.fori_loop(0, 6, some, 0)

    return pl.pallas_call(
        kernel,
        out_shape=[jax.ShapeDtypeStruct((2, 2, n, 16, 512), jnp.float32) for n in (8, 8, 6, 6)],
        in_specs=[VMEM] * 8,
        out_specs=[VMEM] * 4,
        compiler_params=params(2),
        cost_estimate=pl.CostEstimate(flops=0, bytes_accessed=4 << 20, transcendentals=0),
    )(*pieces)


def here(block):
    def kernel(block, out):
        out[...] = block[...]

    return pl.pallas_call(
        kernel,
        out_shape=jax.ShapeDtypeStruct(block.shape, jnp.float32),
        in_specs=[VMEM],
        out_specs=VMEM,
        compiler_params=params(2),
        cost_estimate=pl.CostEstimate(flops=0, bytes_accessed=1 << 17, transcendentals=0),
    )(block)


def last_z(first, second):
    def kernel(first, second, out):
        out[0] = first[:, :, 4:]
        out[1] = second[:, :, 4:]

    return pl.pallas_call(
        kernel,
        out_shape=jax.ShapeDtypeStruct((2, 2, 2, 2, 16, 512), jnp.float32),
        in_specs=[VMEM] * 2,
        out_specs=VMEM,
        compiler_params=params(2),
        cost_estimate=pl.CostEstimate(flops=0, bytes_accessed=1 << 20, transcendentals=0),
    )(first, second)


def both(first, second):
    def kernel(first, second, out):
        out[0] = first[...]
        out[1] = second[...]

    return pl.pallas_call(
        kernel,
        out_shape=jax.ShapeDtypeStruct((2,) + first.shape, jnp.float32),
        in_specs=[VMEM] * 2,
        out_specs=VMEM,
        compiler_params=params(2),
        cost_estimate=pl.CostEstimate(flops=0, bytes_accessed=4 << 20, transcendentals=0),
    )(first, second)


def split_kernel(count_ref, a_ref, hi_ref, lo_ref):
    live = count_ref[0] * 64
    column = lax.broadcasted_iota(jnp.int32, (64, 1024), 1)

    def step(i, _):
        rows = pl.ds(pl.multiple_of(i * 64, 64), 64)
        keep = column < jnp.where(i * 64 < live, live, 0)
        a = jnp.where(keep, a_ref[rows, :], 0.0)
        hi = a.astype(jnp.bfloat16)
        hi_ref[rows, :] = hi
        lo_ref[rows, :] = (a - hi.astype(jnp.float32)).astype(jnp.bfloat16)
        return 0

    lax.fori_loop(0, 16, step, 0)


def split(counts, a):
    return pl.pallas_call(
        split_kernel,
        in_specs=[SMEM, VMEM],
        out_specs=[VMEM] * 2,
        out_shape=[jax.ShapeDtypeStruct((1024, 1024), jnp.bfloat16)] * 2,
        compiler_params=params(2),
        cost_estimate=pl.CostEstimate(flops=4 << 20, bytes_accessed=8 << 20, transcendentals=0),
    )(counts, a)


PIECES = (
    (0, 0, None),
    (0, 1, None),
    (3, 0, None),
    (1, 1, None),
    (1, 0, True),
    (3, 1, True),
    (1, 0, False),
    (3, 1, False),
    (2, 0, None),
    (2, 1, None),
)


def collect(pieces, kinds, dom, slot_of, raw):
    core, y_me, x_me, z_me = coordinates()
    for t in range(32):
        slot_of[t] = 16
    for k in range(16):
        slot_of[dom[k]] = k
    parts = []
    for piece, (other, *which) in zip(pieces, kinds):
        parts += [(piece.at[n] if len(which) > 1 else piece, other, i) for n, i in enumerate(which)]
    for piece, other, i in parts:
        away, pair, mine = PIECES[i]
        at = 1 - core if other else core
        far = (jnp.where(at == 0, x_me, y_me) + away) & 3
        parity = z_me & 1

        def tiles(n, _):
            q = n if mine is None else jnp.where(n < 2, n, 2 + parity) if mine else 3 - parity
            for m in range(2):
                major = (jnp.where(at == 0, y_me, x_me) + 2 * pair + m) & 3
                y, x = jnp.where(at == 0, major, far), jnp.where(at == 0, far, major)
                to = slot_of[(y & 1) * 16 + x * 4 + q] * 64
                for s in range(2):
                    for h in range(2):
                        rows = pl.ds(pl.multiple_of(to + s * 32 + h * 16, 16), 16)
                        raw[at, y >> 1, rows, :] = piece[m, h, n * 2 + s]
            return 0

        lax.fori_loop(0, piece.shape[2] // 2, tiles, 0)


def collect_early(dom, pieces, kinds):
    def kernel(dom, *refs):
        collect(refs[:-2], kinds, dom, refs[-1], refs[-2])

    return pl.pallas_call(
        kernel,
        in_specs=[SMEM] + [VMEM] * len(pieces),
        out_specs=VMEM,
        out_shape=jax.ShapeDtypeStruct((2, 2, 1088, 512), jnp.float32),
        scratch_shapes=[pltpu.SMEM((32,), jnp.int32)],
        compiler_params=params(2),
        cost_estimate=pl.CostEstimate(flops=0, bytes_accessed=48 << 20, transcendentals=0),
    )(dom, *pieces)


def product_kernel(kinds, dom, cnt, ahi, alo, _, *refs):
    count = len(kinds)
    pieces, out_hbm, raw, (b, out, slot_of, sem) = refs[:count], refs[count], refs[count + 1], refs[count + 2 :]

    def build(n, slot, rows):
        for m in range(2):
            first = n * 4 + m * 2
            c0, c1 = dom[first], dom[first + 1]

            def read(c):
                group, at = c >> 3, pl.multiple_of(((c >> 1) & 3) * 128, 128)
                return raw[group & 1, group >> 1, rows, pl.ds(at, 128)]

            left, right = pltpu.roll(read(c0), (c0 & 1) * 64, 1), pltpu.roll(read(c1), 64 - (c1 & 1) * 64, 1)
            live0, live1 = jnp.where(first < cnt[0], 64, 0), jnp.where(first + 1 < cnt[0], 128, 0)
            lane = lax.broadcasted_iota(jnp.int32, left.shape, 1)
            keep = (lane < live0) | ((lane >= 64) & (lane < live1))
            value = jnp.where(keep, jnp.where(lane < 64, left, right), 0.0)
            hi = value.astype(jnp.bfloat16)
            b[slot, 0, rows, m * 128 : m * 128 + 128] = hi
            b[slot, 1, rows, m * 128 : m * 128 + 128] = (value - hi.astype(jnp.float32)).astype(jnp.bfloat16)

    collect(pieces, kinds, dom, slot_of, raw)

    def first_build(i, _):
        build(0, 0, pl.ds(pl.multiple_of(i * 64, 64), 64))
        return 0

    lax.fori_loop(0, 16, first_build, 0)

    def written(n, slot):
        columns = pl.ds(pl.multiple_of(n * 256, 256), 256)
        return pltpu.make_async_copy(out.at[slot], out_hbm.at[:, columns], sem.at[slot])

    def multiply(n, _):
        slot = n & 1

        @pl.when(n >= 2)
        def _():
            written(n - 2, slot).wait()

        total = jnp.dot(ahi[...], b[slot, 0], preferred_element_type=jnp.float32)
        total += jnp.dot(ahi[...], b[slot, 1], preferred_element_type=jnp.float32)
        total += jnp.dot(alo[...], b[slot, 0], preferred_element_type=jnp.float32)
        out[slot] = total
        build((n + 1) & 3, 1 - slot, pl.ds(0, 1024))
        written(n, slot).start()
        return 0

    lax.fori_loop(0, 4, multiply, 0)
    written(2, 0).wait()
    written(3, 1).wait()


def product(dom, cnt, ahi, alo, raw, pieces, kinds):
    return pl.pallas_call(
        functools.partial(product_kernel, kinds),
        in_specs=[SMEM] * 2 + [VMEM] * (3 + len(pieces)),
        out_specs=[ANY, VMEM],
        out_shape=[jax.ShapeDtypeStruct((1024, 1024), jnp.float32), jax.ShapeDtypeStruct(raw.shape, raw.dtype)],
        scratch_shapes=[
            pltpu.VMEM((2, 2, 1024, 256), jnp.bfloat16),
            pltpu.VMEM((2, 1024, 256), jnp.float32),
            pltpu.SMEM((32,), jnp.int32),
            pltpu.SemaphoreType.DMA((2,)),
        ],
        input_output_aliases={4: 1},
        compiler_params=params(11),
        cost_estimate=pl.CostEstimate(flops=6 << 30, bytes_accessed=20 << 20, transcendentals=0),
    )(dom, cnt, ahi, alo, raw, *pieces)[0]


def shards(amplitudes, domain, counts, integrals):
    Z = ("z", "z")
    got = {0: integrals}
    for d in (1, -1, 2, -2):
        got[d] = fetch(integrals, Z, d)
    got[2], got[-2], got[0] = tie(got[2], got[-2], here(integrals))
    got[3], got[-3] = fetch(got[2], Z, 1), fetch(got[-2], Z, -1)
    top, low = fetch(got[2][:16], Z, 2), fetch(got[-2][16:], Z, -2)
    A, B = by_z([got[d] for d in (0, 1, -1, 2, -2, 3, -3)] + [top, low])

    YX = ("y", "x")
    a3, b1 = fetch(A, YX, -1), fetch(B, YX, 1)
    a1, b3 = fetch(A, YX, 1), fetch(B, YX, -1)
    a2, b2 = fetch(a3, YX, -1), fetch(b1, YX, 1)

    first, second, first_mine, second_mine = by_yx([A, B, a1, b1, a2, b2, a3, b3])

    XY = ("x", "y")
    swap = lambda piece: lax.ppermute(piece, AXES, moved([{"core": 1}] * 2))
    first3, second1 = fetch(first, XY, -1), fetch(second, XY, 1)
    first1, second3 = fetch(first_mine, XY, 1), fetch(second_mine, XY, -1)
    other_first = swap(first)
    second, other_first = tie(second, other_first)
    other_second = swap(second)
    ahi, alo = split(counts, amplitudes[0])
    first3, second1, other_first, other_second, ahi, alo = tie(first3, second1, other_first, other_second, ahi, alo)
    first2, second2 = fetch(first3, XY, -1), fetch(second1, XY, 1)
    rest = lax.ppermute(last_z(first1, second3), AXES, moved([{"z": -1}, {"z": 1}]))

    own = [first, second, first3, second1, first1, second3]
    other = [other_first, other_second, swap(both(first3, second1)), swap(both(first1, second3))]
    early = [(0, i) for i in range(6)] + [(1, 0), (1, 1), (1, 2, 3), (1, 4, 5)]
    raw = collect_early(domain[0], own + other, early)
    last = [rest, first2, second2]
    late = [(c, *which) for c in range(2) for which in ((6, 7), (8,), (9,))]
    return product(domain[0], counts, ahi, alo, raw, last + [swap(piece) for piece in last], late)[None]


def solution(mesh):
    fine = Mesh(mesh.devices.reshape(SIZES), AXES)
    whole = P(AXES, None, None)
    return jax.shard_map(
        shards,
        mesh=fine,
        in_specs=(whole, P(AXES, None), P(AXES), P(("yl", "x", "z"), ("yh", "core"))),
        out_specs=whole,
        check_vma=False,
    )
```
